32 devices in a mesh: groups: 2 (over x), wide: 16 (over z, y, core).
Axes of the slice: x: 2, y: 2, z: 4, core: 2. Of those that a mesh axis runs over, the one named last changes fastest.
Arguments:
- tokens: bfloat16 [512, 6144], P(('groups', 'wide')), parts along dimension 0, may hold values from -6 to 6
- target: bfloat16 [512, 6144], P(('groups', 'wide')), parts along dimension 0, may hold values from -6 to 6
- norm_gain: float32 [6144], replicated, may hold values from 0.25 to 1.75
- up_weight: bfloat16 [6144, 12288], P(None, 'wide'), may hold values from -0.078125 to 0.078125
- down_weight: bfloat16 [12288, 6144], P('wide'), may hold values from -0.0546875 to 0.0546875
- model_codes: int32 [4, 6144], P('groups'), parts along dimension 0, may hold values from 0 to 1073741823
- hidden_codes: int32 [4, 12288], P('groups', 'wide'), parts along dimension 0, may hold values from 0 to 1073741823
Outputs:
- hessian_up: bfloat16 [12288, 12288], P('groups', 'wide'), parts along dimension 0
- hessian_down: bfloat16 [24576, 6144], P(('groups', 'wide')), parts along dimension 0
- quadratic_form: float32 [2], P('groups'), parts along dimension 0
The draws below stay inside these ranges and needn't reach their ends.
There are 2 independent parts, one for each index of `groups`. The reference program is written for one: setup_inputs(seed, part) draws one part's arguments, and reference() takes and returns one part's arrays. A program takes and returns all parts, laid end to end along the dimension named above; an argument that names none is the same for every part. Nothing has to cross between parts.
Inputs may be any that keep to these rules, and one draw needn't show every extreme that they name: `model_codes`: each entry holds 30 random bits. `hidden_codes`: each entry holds 30 random bits.
All inputs are finite; a program needn't handle non-finite values.
Results may differ from the reference program's by a relative error of at most 0.0076.
Values may be sent and summed in bfloat16 or wider, within the bound.
A program may use at most 192 MiB of HBM per device.

```python
import jax
import jax.numpy as jnp
from jax import lax

D = 6144
FF = 12288
TOKENS = 256


def touch_ends(values, rng, smallest, top_value):
    longest = values.shape.index(max(values.shape))
    spots = []
    for shift in (0, 1):
        where = [jax.random.randint(jax.random.fold_in(rng, axis), (), 0, length) for axis, length in enumerate(values.shape)]
        where[longest] = (where[longest] + shift) % values.shape[longest]
        spots.append(tuple(where))
    return values.at[spots[0]].set(smallest).at[spots[1]].set(top_value)


def steps_of(rng, dims, shards, smallest, largest):
    level, own = 1.0, jax.random.fold_in(rng, 6)
    for dim, parts in shards:
        steps = jnp.exp(jax.random.uniform(jax.random.fold_in(own, dim), (parts,), jnp.float32, smallest / len(shards), largest / len(shards)))
        level = level * jnp.repeat(steps, dims[dim] // parts).reshape([-1 if axis == dim else 1 for axis in range(len(dims))])
    return level


def noise(key, shape, width, reach, shards=(), dtype=jnp.bfloat16):
    entries = jax.random.normal(key, shape, jnp.float32) * width
    if len(shards) > 0:
        entries = steps_of(key, shape, shards, -0.22, 0.18) * entries
    return jnp.clip(entries, min=-reach, max=reach).astype(dtype)


def setup_inputs(seed: int = 0, part: int = 0) -> dict:
    key_of = jax.random.split(jax.random.key(seed), 8)
    part_keys = jax.random.split(jax.random.fold_in(key_of[7], part), 8)
    tokens = noise(part_keys[0], (TOKENS, D), 1.0, 6.0, ((0, 16),))
    target = noise(part_keys[1], (TOKENS, D), 1.0, 6.0, ((0, 16),))
    norm_gain = jnp.clip(1.0 + 0.15 * jax.random.normal(key_of[2], (D,), jnp.float32), 0.25, 1.75)
    up_weight = noise(key_of[3], (D, FF), D ** -0.5, 0.078125, ((1, 16),))
    down_weight = noise(key_of[4], (FF, D), FF ** -0.5, 0.0546875, ((0, 16),))
    model_codes = touch_ends(jax.random.randint(part_keys[5], (2, D), 0, 1073741824), jax.random.fold_in(part_keys[5], 1), 0, 1073741823).astype(jnp.int32)
    hidden_codes = touch_ends(jax.random.randint(part_keys[6], (2, FF), 0, 1073741824), jax.random.fold_in(part_keys[6], 1), 0, 1073741823).astype(jnp.int32)
    return dict(tokens=tokens, target=target, norm_gain=norm_gain, up_weight=up_weight, down_weight=down_weight, model_codes=model_codes, hidden_codes=hidden_codes)


def normalize(rows, norm_gain):
    wide_rows = rows.astype(jnp.float32)
    center = lax.optimization_barrier(jnp.mean(wide_rows, axis=1, keepdims=True))
    spread = lax.optimization_barrier(jnp.mean((wide_rows - center) ** 2, axis=1, keepdims=True))
    return ((wide_rows - center) * lax.rsqrt(spread + 1e-06) * norm_gain).astype(jnp.bfloat16)

def bit_parity(values):
    folded = jnp.bitwise_xor(values, jnp.right_shift(values, 16))
    folded = jnp.bitwise_xor(folded, jnp.right_shift(folded, 8))
    folded = jnp.bitwise_xor(folded, jnp.right_shift(folded, 4))
    folded = jnp.bitwise_xor(folded, jnp.right_shift(folded, 2))
    folded = jnp.bitwise_xor(folded, jnp.right_shift(folded, 1))
    return jnp.bitwise_and(folded, 1)

def probe_signs(row_codes, column_codes, factor):
    shared = jnp.bitwise_and(row_codes[:, None], column_codes[None, :])
    parity = bit_parity(shared)
    return ((1 - 2 * parity).astype(jnp.float32) * factor).astype(jnp.bfloat16)

def gelu_parts(preact):
    density = jnp.exp(-0.5 * preact * preact) * 0.3989422804014327
    cumulative = 0.5 * (1.0 + jax.scipy.special.erf(preact * 0.7071067811865476))
    return (preact * cumulative, cumulative + preact * density, density * (2.0 - preact * preact))

def contract_last(left, right):
    return lax.dot_general(left, right, (((1,), (1,)), ((), ())), preferred_element_type=jnp.float32)

def contract_first(left, right):
    return lax.dot_general(left, right, (((0,), (0,)), ((), ())), preferred_element_type=jnp.float32)

def reference(tokens, target, norm_gain, up_weight, down_weight, model_codes, hidden_codes):
    normed = normalize(tokens, norm_gain)
    probe_up = probe_signs(model_codes[0], hidden_codes[0], D ** (-0.5))
    probe_down = probe_signs(hidden_codes[1], model_codes[1], FF ** (-0.5))
    preact = jnp.dot(normed, up_weight, preferred_element_type=jnp.float32)
    tangent = jnp.dot(normed, probe_up, preferred_element_type=jnp.float32)
    hidden_f32, first_slope, second_slope = gelu_parts(preact)
    hidden_act = hidden_f32.astype(jnp.bfloat16)
    hidden_tan = (first_slope * tangent).astype(jnp.bfloat16)
    outputs = tokens.astype(jnp.float32) + jnp.dot(hidden_act, down_weight, preferred_element_type=jnp.float32)
    doutputs = jnp.dot(hidden_tan, down_weight, preferred_element_type=jnp.float32) + jnp.dot(hidden_act, probe_down, preferred_element_type=jnp.float32)
    residual_scaled = ((outputs - target.astype(jnp.float32)) / TOKENS).astype(jnp.bfloat16)
    tangent_scaled = (doutputs / TOKENS).astype(jnp.bfloat16)
    back_hidden = contract_last(residual_scaled, down_weight)
    dback_hidden = contract_last(tangent_scaled, down_weight) + contract_last(residual_scaled, probe_down)
    curvature = (second_slope * tangent * back_hidden + first_slope * dback_hidden).astype(jnp.bfloat16)
    hessian_f32_up = contract_first(normed, curvature)
    hessian_f32_down = contract_first(hidden_tan, residual_scaled) + contract_first(hidden_act, tangent_scaled)
    quadratic_form = jnp.sum(probe_up.astype(jnp.float32) * hessian_f32_up) + jnp.sum(probe_down.astype(jnp.float32) * hessian_f32_down)
    return (hessian_f32_up.astype(jnp.bfloat16), hessian_f32_down.astype(jnp.bfloat16), jnp.reshape(quadratic_form, (1,)))
```

```python
import functools

import jax
import jax.numpy as jnp
from jax import lax
from jax.sharding import PartitionSpec as P

D = 6144
FF = 12288


def normalize(rows, norm_gain):
    wide_rows = rows.astype(jnp.float32)
    center = jnp.mean(wide_rows, axis=1, keepdims=True)
    spread = jnp.mean((wide_rows - center) ** 2, axis=1, keepdims=True)
    return ((wide_rows - center) * lax.rsqrt(spread + 1e-06) * norm_gain).astype(jnp.bfloat16)


def probe_signs(row_codes, column_codes, factor):
    shared = jnp.bitwise_and(row_codes[:, None], column_codes[None, :])
    odd = jnp.bitwise_and(lax.population_count(shared), 1) == 1
    size = jnp.asarray(factor, jnp.float32)
    return jnp.where(odd, -size, size).astype(jnp.bfloat16)


def gelu_parts(preact):
    density = jnp.exp(-0.5 * preact * preact) * 0.3989422804014327
    cumulative = 0.5 * (1.0 + jax.scipy.special.erf(preact * 0.7071067811865476))
    return (preact * cumulative, cumulative + preact * density, density * (2.0 - preact * preact))


def contract_last(left, right):
    return lax.dot_general(
        left, right, (((1,), (1,)), ((), ())), preferred_element_type=jnp.float32
    )


def contract_first(left, right):
    return lax.dot_general(
        left, right, (((0,), (0,)), ((), ())), preferred_element_type=jnp.float32
    )


def swap(value, bit, size):
    pairs = [(i, i ^ (1 << bit)) for i in range(size)]
    return lax.ppermute(value, "wide", pairs)


def stage_orders(bits):
    first = list(range(bits))
    second = list(first)
    if bits > 2:
        second[1], second[2] = first[2], first[1]
    return first, second


def gather_part(rows, order, size):
    bits = len(order)
    value = rows.reshape((1,) * bits + rows.shape)
    for bit in reversed(order):
        value = lax.concatenate([value, swap(value, bit, size)], bits - 1 - bit)
    return value.reshape(size * rows.shape[0], rows.shape[1])


def gather_rows(rows, size):
    half = rows.shape[1] // 2
    orders = stage_orders(size.bit_length() - 1)
    return jnp.concatenate(
        [
            gather_part(rows[:, :half], orders[0], size),
            gather_part(rows[:, half:], orders[1], size),
        ],
        axis=1,
    )


def scatter_part(total, order, size):
    bits = len(order)
    rows = total.shape[0] // size
    value = total.reshape((2,) * bits + (rows, total.shape[1]))
    for bit in order:
        axis = bits - 1 - bit
        kept = lax.slice_in_dim(value, 0, 1, axis=axis)
        sent = lax.slice_in_dim(value, 1, 2, axis=axis).astype(jnp.bfloat16)
        value = kept + swap(sent, bit, size).astype(jnp.float32)
    return value.reshape(rows, total.shape[1])


def scatter_rows(total, size):
    half = total.shape[1] // 2
    orders = stage_orders(size.bit_length() - 1)
    return jnp.concatenate(
        [
            scatter_part(total[:, :half], orders[0], size),
            scatter_part(total[:, half:], orders[1], size),
        ],
        axis=1,
    )


def add_over(value, size):
    for bit in range(size.bit_length() - 1):
        value = value + swap(value, bit, size)
    return value


def on_device(
    size, tokens, target, norm_gain, up_weight, down_weight, model_codes, hidden_codes
):
    normed = gather_rows(normalize(tokens, norm_gain), size)
    total_rows = normed.shape[0]
    probe_up = lax.optimization_barrier(probe_signs(model_codes[0], hidden_codes[0], D ** (-0.5)))
    probe_down = lax.optimization_barrier(
        probe_signs(hidden_codes[1], model_codes[1], FF ** (-0.5))
    )
    preact = jnp.dot(normed, up_weight, preferred_element_type=jnp.float32)
    hidden_f32, first_slope, second_slope = gelu_parts(preact)
    hidden_act = hidden_f32.astype(jnp.bfloat16)
    forward_part = jnp.dot(hidden_act, down_weight, preferred_element_type=jnp.float32)
    tangent = jnp.dot(normed, probe_up, preferred_element_type=jnp.float32)
    hidden_tan = (first_slope * tangent).astype(jnp.bfloat16)
    probe_part = jnp.dot(hidden_act, probe_down, preferred_element_type=jnp.float32)
    tangent_part = (
        jnp.dot(hidden_tan, down_weight, preferred_element_type=jnp.float32) + probe_part
    )
    outputs = tokens.astype(jnp.float32) + scatter_rows(forward_part, size)
    residual_scaled = ((outputs - target.astype(jnp.float32)) / total_rows).astype(jnp.bfloat16)
    residual_all = gather_rows(residual_scaled, size)
    tangent_scaled = (scatter_rows(tangent_part, size) / total_rows).astype(jnp.bfloat16)
    tangent_all = gather_rows(tangent_scaled, size)
    back_hidden = contract_last(residual_all, down_weight)
    back_probe = contract_last(residual_all, probe_down)
    dback_hidden = contract_last(tangent_all, down_weight) + back_probe
    curvature = (second_slope * tangent * back_hidden + first_slope * dback_hidden).astype(
        jnp.bfloat16
    )
    local_sum = (
        jnp.sum(tangent * curvature.astype(jnp.float32))
        + jnp.sum(hidden_tan.astype(jnp.float32) * back_probe)
        + jnp.sum(probe_part * tangent_all.astype(jnp.float32))
    )
    quadratic_form = add_over(jnp.reshape(local_sum, (1,)), size)
    hessian_f32_up = contract_first(normed, curvature)
    hessian_f32_down = contract_first(
        jnp.concatenate([hidden_tan, hidden_act], axis=0),
        jnp.concatenate([residual_all, tangent_all], axis=0),
    )
    return (
        hessian_f32_up.astype(jnp.bfloat16),
        hessian_f32_down.astype(jnp.bfloat16),
        quadratic_form,
    )


def solution(mesh):
    return jax.shard_map(
        functools.partial(on_device, mesh.shape["wide"]),
        mesh=mesh,
        in_specs=(
            P(("groups", "wide"), None),
            P(("groups", "wide"), None),
            P(),
            P(None, "wide"),
            P("wide", None),
            P("groups", None),
            P("groups", "wide"),
        ),
        out_specs=(P("groups", "wide"), P(("groups", "wide"), None), P("groups")),
        check_vma=False,
    )
```

```python
import functools

import jax
import jax.numpy as jnp
from jax import lax
from jax.sharding import PartitionSpec as P

D = 6144
FF = 12288


def normalize(rows, norm_gain):
    wide_rows = rows.astype(jnp.float32)
    center = jnp.mean(wide_rows, axis=1, keepdims=True)
    spread = jnp.mean((wide_rows - center) ** 2, axis=1, keepdims=True)
    return ((wide_rows - center) * lax.rsqrt(spread + 1e-06) * norm_gain).astype(jnp.bfloat16)


def probe_signs(row_codes, column_codes, factor):
    shared = jnp.bitwise_and(row_codes[:, None], column_codes[None, :])
    odd = jnp.bitwise_and(lax.population_count(shared), 1) == 1
    size = jnp.asarray(factor, jnp.float32)
    return jnp.where(odd, -size, size).astype(jnp.bfloat16)


def gelu_parts(preact):
    density = jnp.exp(-0.5 * preact * preact) * 0.3989422804014327
    cumulative = 0.5 * (1.0 + jax.scipy.special.erf(preact * 0.7071067811865476))
    return (preact * cumulative, cumulative + preact * density, density * (2.0 - preact * preact))


def contract_last(left, right):
    return lax.dot_general(
        left, right, (((1,), (1,)), ((), ())), preferred_element_type=jnp.float32
    )


def contract_first(left, right):
    return lax.dot_general(
        left, right, (((0,), (0,)), ((), ())), preferred_element_type=jnp.float32
    )


def swap(value, bit, size):
    pairs = [(i, i ^ (1 << bit)) for i in range(size)]
    return lax.ppermute(value, "wide", pairs)


def stage_orders(bits):
    first = list(range(bits))
    second = list(first)
    if bits > 2:
        second[1], second[2] = first[2], first[1]
    return first, second


def spread(rows, bits):
    return rows.reshape((1,) * bits + rows.shape)


def gather_stage(value, bit, bits, size):
    return lax.concatenate([value, swap(value, bit, size)], bits - 1 - bit)


def split_rows(total, bits, size):
    return total.reshape((2,) * bits + (total.shape[0] // size, total.shape[1]))


def scatter_stage(value, bit, bits, size):
    axis = bits - 1 - bit
    kept = lax.slice_in_dim(value, 0, 1, axis=axis)
    sent = lax.slice_in_dim(value, 1, 2, axis=axis).astype(jnp.bfloat16)
    return kept + swap(sent, bit, size).astype(jnp.float32)


def add_over(value, size):
    for bit in range(size.bit_length() - 1):
        value = value + swap(value, bit, size)
    return value


def on_device(
    size, tokens, target, norm_gain, up_weight, down_weight, model_codes, hidden_codes
):
    bits = size.bit_length() - 1
    orders = stage_orders(bits)
    own_rows, width = tokens.shape
    total_rows = own_rows * size

    probes = [
        lambda: probe_signs(model_codes[0], hidden_codes[0], D ** (-0.5)),
        lambda: probe_signs(hidden_codes[1], model_codes[1], FF ** (-0.5)),
    ]
    made = []
    own = normalize(tokens, norm_gain)
    halves = [spread(own[:, : width // 2], bits), spread(own[:, width // 2 :], bits)]
    for stage in reversed(range(bits)):
        if stage < 2:
            joined = lax.optimization_barrier((halves[0], halves[1], probes[stage]()))
            halves = [joined[0], joined[1]]
            made.append(joined[2])
        halves = [
            gather_stage(half, order[stage], bits, size) for half, order in zip(halves, orders)
        ]
    probe_down, probe_up = made
    normed = jnp.concatenate([half.reshape(total_rows, width // 2) for half in halves], axis=1)

    preact = jnp.dot(normed, up_weight, preferred_element_type=jnp.float32)
    hidden_f32, first_slope, second_slope = gelu_parts(preact)
    hidden_act = hidden_f32.astype(jnp.bfloat16)
    forward_part = jnp.dot(hidden_act, down_weight, preferred_element_type=jnp.float32)
    forward_sum = scatter_stage(split_rows(forward_part, bits, size), orders[0][0], bits, size)
    tangent = jnp.dot(normed, probe_up, preferred_element_type=jnp.float32)
    hidden_tan = (first_slope * tangent).astype(jnp.bfloat16)
    tangent_part = jnp.dot(
        hidden_tan, down_weight, preferred_element_type=jnp.float32
    ) + jnp.dot(hidden_act, probe_down, preferred_element_type=jnp.float32)
    forward_sum, tangent_part = lax.optimization_barrier((forward_sum, tangent_part))
    tangent_sum = scatter_stage(split_rows(tangent_part, bits, size), orders[1][0], bits, size)
    for stage in range(1, bits):
        forward_sum = scatter_stage(forward_sum, orders[0][stage], bits, size)
        tangent_sum = scatter_stage(tangent_sum, orders[1][stage], bits, size)
    outputs = tokens.astype(jnp.float32) + forward_sum.reshape(own_rows, width)
    doutputs = tangent_sum.reshape(own_rows, width)
    residual_own = ((outputs - target.astype(jnp.float32)) / total_rows).astype(jnp.bfloat16)
    tangent_own = (doutputs / total_rows).astype(jnp.bfloat16)
    residual_all, tangent_all = spread(residual_own, bits), spread(tangent_own, bits)
    for stage in reversed(range(bits)):
        residual_all = gather_stage(residual_all, orders[0][stage], bits, size)
        tangent_all = gather_stage(tangent_all, orders[1][stage], bits, size)
    scaled = lax.optimization_barrier(
        jnp.concatenate(
            [residual_all.reshape(total_rows, width), tangent_all.reshape(total_rows, width)],
            axis=0,
        )
    )
    hidden = lax.optimization_barrier(jnp.concatenate([hidden_tan, hidden_act], axis=0))

    back = contract_last(scaled, down_weight)
    back_hidden, back_tangent = back[:total_rows], back[total_rows:]
    back_probe = contract_last(scaled[:total_rows], probe_down)
    curvature = (
        second_slope * tangent * back_hidden + first_slope * (back_tangent + back_probe)
    ).astype(jnp.bfloat16)
    local_sum = jnp.sum(
        tangent * curvature.astype(jnp.float32)
        + hidden_tan.astype(jnp.float32) * (back_probe - back_tangent)
    ) + jnp.sum(doutputs * tangent_own.astype(jnp.float32))
    quadratic_form = add_over(jnp.reshape(local_sum, (1,)), size)
    hessian_f32_up = contract_first(normed, curvature)
    hessian_f32_down = contract_first(hidden, scaled)
    return (
        hessian_f32_up.astype(jnp.bfloat16),
        hessian_f32_down.astype(jnp.bfloat16),
        quadratic_form,
    )


def solution(mesh):
    return jax.shard_map(
        functools.partial(on_device, mesh.shape["wide"]),
        mesh=mesh,
        in_specs=(
            P(("groups", "wide"), None),
            P(("groups", "wide"), None),
            P(),
            P(None, "wide"),
            P("wide", None),
            P("groups", None),
            P("groups", "wide"),
        ),
        out_specs=(P("groups", "wide"), P(("groups", "wide"), None), P("groups")),
        check_vma=False,
    )
```

```python
import functools

import jax
import jax.numpy as jnp
from jax import lax
from jax.sharding import PartitionSpec as P

D = 6144
FF = 12288


def normalize(rows, norm_gain):
    wide_rows = rows.astype(jnp.float32)
    center = jnp.mean(wide_rows, axis=1, keepdims=True)
    spread = jnp.mean((wide_rows - center) ** 2, axis=1, keepdims=True)
    return ((wide_rows - center) * lax.rsqrt(spread + 1e-06) * norm_gain).astype(jnp.bfloat16)


def probe_signs(row_codes, column_codes, factor):
    shared = jnp.bitwise_and(row_codes[:, None], column_codes[None, :])
    odd = jnp.bitwise_and(lax.population_count(shared), 1) == 1
    size = jnp.asarray(factor, jnp.float32)
    return jnp.where(odd, -size, size).astype(jnp.bfloat16)


def gelu_parts(preact):
    density = jnp.exp(-0.5 * preact * preact) * 0.3989422804014327
    cumulative = 0.5 * (1.0 + jax.scipy.special.erf(preact * 0.7071067811865476))
    return (preact * cumulative, cumulative + preact * density, density * (2.0 - preact * preact))


def contract_last(left, right):
    return lax.dot_general(
        left, right, (((1,), (1,)), ((), ())), preferred_element_type=jnp.float32
    )


def contract_first(left, right):
    return lax.dot_general(
        left, right, (((0,), (0,)), ((), ())), preferred_element_type=jnp.float32
    )


def swap_with(value, mask, size):
    pairs = [(i, i ^ mask) for i in range(size)]
    return lax.ppermute(value, "wide", pairs)


def swap(value, bit, size):
    return swap_with(value, 1 << bit, size)


def stage_orders(bits):
    first = list(range(bits))
    second = list(first)
    if bits > 2:
        second[1], second[2] = first[2], first[1]
    return first, second


def spread(rows, bits):
    return rows.reshape((1,) * bits + rows.shape)


def gather_stage(value, bit, bits, size):
    return lax.concatenate([value, swap(value, bit, size)], bits - 1 - bit)


def split_rows(total, bits, size):
    return total.reshape((2,) * bits + (total.shape[0] // size, total.shape[1]))


def scatter_stage(value, bit, bits, size):
    axis = bits - 1 - bit
    kept = lax.slice_in_dim(value, 0, 1, axis=axis)
    sent = lax.slice_in_dim(value, 1, 2, axis=axis).astype(jnp.bfloat16)
    return kept + swap(sent, bit, size).astype(jnp.float32)


def add_over(value, size, beside):
    results = []
    bit = 0
    while bit < size.bit_length() - 1:
        if beside:
            operand, product = beside.pop(0)
            value, operand = lax.optimization_barrier((value, operand))
            results.append(product(operand))
        if 2 << bit < size:
            near = swap_with(value, 1 << bit, size)
            far = (swap_with(value, 2 << bit, size), swap_with(value, 3 << bit, size))
        else:
            near, far = swap_with(value, 1 << bit, size), None
        if bit < 2 * len(results):
            near, far, results[-1] = lax.optimization_barrier((near, far, results[-1]))
        value = value + near if far is None else (value + near) + (far[0] + far[1])
        bit += 2
    return value, results + [product(operand) for operand, product in beside]


def on_device(
    size, tokens, target, norm_gain, up_weight, down_weight, model_codes, hidden_codes
):
    bits = size.bit_length() - 1
    orders = stage_orders(bits)
    own_rows, width = tokens.shape
    total_rows = own_rows * size

    probes = [
        lambda: probe_signs(model_codes[0], hidden_codes[0], D ** (-0.5)),
        lambda: probe_signs(hidden_codes[1], model_codes[1], FF ** (-0.5)),
    ]
    made = []
    own = normalize(tokens, norm_gain)
    halves = [spread(own[:, : width // 2], bits), spread(own[:, width // 2 :], bits)]
    for stage in reversed(range(bits)):
        if stage < 2:
            joined = lax.optimization_barrier((halves[0], halves[1], probes[stage]()))
            halves = [joined[0], joined[1]]
            made.append(joined[2])
        halves = [
            gather_stage(half, order[stage], bits, size) for half, order in zip(halves, orders)
        ]
    probe_down, probe_up = made
    normed = jnp.concatenate([half.reshape(total_rows, width // 2) for half in halves], axis=1)

    preact = jnp.dot(normed, up_weight, preferred_element_type=jnp.float32)
    hidden_f32, first_slope, second_slope = gelu_parts(preact)
    hidden_act = hidden_f32.astype(jnp.bfloat16)
    forward_part = jnp.dot(hidden_act, down_weight, preferred_element_type=jnp.float32)
    tangent = jnp.dot(normed, probe_up, preferred_element_type=jnp.float32)
    hidden_tan = (first_slope * tangent).astype(jnp.bfloat16)
    tangent_part = jnp.dot(
        hidden_tan, down_weight, preferred_element_type=jnp.float32
    ) + jnp.dot(hidden_act, probe_down, preferred_element_type=jnp.float32)

    def cut(total):
        half = width // 2
        return [split_rows(total[:, :half], bits, size), split_rows(total[:, half:], bits, size)]

    def whole(pair):
        return jnp.concatenate([part.reshape(-1, width // 2) for part in pair], axis=1)

    def advance(pair, step):
        if step < bits:
            return [
                scatter_stage(part, order[step], bits, size) for part, order in zip(pair, orders)
            ]
        return [
            gather_stage(part, order[2 * bits - 1 - step], bits, size)
            for part, order in zip(pair, orders)
        ]

    def halves_of(rows):
        half = width // 2
        return [spread(rows[:, :half], bits), spread(rows[:, half:], bits)]

    lag = 2
    steps = 2 * bits
    output_pair, tangent_pair = cut(forward_part), tangent_part
    for tick in range(steps + lag):
        extra = None
        if tick == steps:
            residual_all = whole(output_pair)
            extra = contract_last(residual_all, down_weight)
        if tick == steps + 1:
            extra = (
                contract_last(residual_all, probe_down),
                jnp.concatenate([hidden_tan, hidden_act], axis=0),
            )
        if tick == bits:
            outputs = tokens.astype(jnp.float32) + whole(output_pair)
            residual_own = (outputs - target.astype(jnp.float32)) / total_rows
            output_pair = halves_of(residual_own.astype(jnp.bfloat16))
        if tick == lag:
            tangent_pair = cut(tangent_pair)
        if tick == lag + bits:
            doutputs = whole(tangent_pair)
            tangent_own = (doutputs / total_rows).astype(jnp.bfloat16)
            tangent_pair = halves_of(tangent_own)
        if tick < steps:
            output_pair = advance(output_pair, tick)
        if tick >= lag:
            tangent_pair = advance(tangent_pair, tick - lag)
        if tick < steps:
            output_pair, tangent_pair = lax.optimization_barrier((output_pair, tangent_pair))
        else:
            residual_all, tangent_pair, extra = lax.optimization_barrier(
                (residual_all, tangent_pair, extra)
            )
            if tick == steps:
                back_hidden = extra
            else:
                back_probe, hidden = extra
    scaled = lax.optimization_barrier(
        jnp.concatenate([residual_all, whole(tangent_pair)], axis=0)
    )

    back_tangent = contract_last(scaled[total_rows:], down_weight)
    curvature = (
        second_slope * tangent * back_hidden + first_slope * (back_tangent + back_probe)
    ).astype(jnp.bfloat16)
    local_sum = jnp.sum(
        tangent * curvature.astype(jnp.float32)
        + hidden_tan.astype(jnp.float32) * (back_probe - back_tangent)
    ) + jnp.sum(doutputs * tangent_own.astype(jnp.float32))
    quadratic_form, (hessian_down, hessian_up) = add_over(
        jnp.reshape(local_sum, (1,)),
        size,
        [
            (hidden, lambda left: contract_first(left, scaled).astype(jnp.bfloat16)),
            (curvature, lambda right: contract_first(normed, right).astype(jnp.bfloat16)),
        ],
    )
    return hessian_up, hessian_down, quadratic_form


def solution(mesh):
    return jax.shard_map(
        functools.partial(on_device, mesh.shape["wide"]),
        mesh=mesh,
        in_specs=(
            P(("groups", "wide"), None),
            P(("groups", "wide"), None),
            P(),
            P(None, "wide"),
            P("wide", None),
            P("groups", None),
            P("groups", "wide"),
        ),
        out_specs=(P("groups", "wide"), P(("groups", "wide"), None), P("groups")),
        check_vma=False,
    )
```

```python
import functools

import jax
import jax.numpy as jnp
from jax import lax
from jax.sharding import PartitionSpec as P

D = 6144
FF = 12288


def normalize(rows, norm_gain):
    wide_rows = rows.astype(jnp.float32)
    center = jnp.mean(wide_rows, axis=1, keepdims=True)
    spread = jnp.mean((wide_rows - center) ** 2, axis=1, keepdims=True)
    return ((wide_rows - center) * lax.rsqrt(spread + 1e-06) * norm_gain).astype(jnp.bfloat16)


def probe_signs(row_codes, column_codes, factor):
    shared = jnp.bitwise_and(row_codes[:, None], column_codes[None, :])
    odd = jnp.bitwise_and(lax.population_count(shared), 1) == 1
    size = jnp.asarray(factor, jnp.float32)
    return jnp.where(odd, -size, size).astype(jnp.bfloat16)


def gelu_parts(preact):
    density = jnp.exp(-0.5 * preact * preact) * 0.3989422804014327
    cumulative = 0.5 * (1.0 + jax.scipy.special.erf(preact * 0.7071067811865476))
    return (preact * cumulative, cumulative + preact * density, density * (2.0 - preact * preact))


def contract_last(left, right):
    return lax.dot_general(
        left, right, (((1,), (1,)), ((), ())), preferred_element_type=jnp.float32
    )


def contract_first(left, right):
    return lax.dot_general(
        left, right, (((0,), (0,)), ((), ())), preferred_element_type=jnp.float32
    )


def swap(value, bit, size):
    pairs = [(i, i ^ (1 << bit)) for i in range(size)]
    return lax.ppermute(value, "wide", pairs)


def stage_orders(bits):
    first = list(range(bits))
    second = list(first)
    if bits > 2:
        second[1], second[2] = first[2], first[1]
    return first, second


def spread(rows, bits):
    return rows.reshape((1,) * bits + rows.shape)


def gather_stage(value, bit, bits, size):
    return lax.concatenate([value, swap(value, bit, size)], bits - 1 - bit)


def split_rows(total, bits, size):
    return total.reshape((2,) * bits + (total.shape[0] // size, total.shape[1]))


def scatter_stage(value, bit, bits, size):
    axis = bits - 1 - bit
    kept = lax.slice_in_dim(value, 0, 1, axis=axis)
    sent = lax.slice_in_dim(value, 1, 2, axis=axis).astype(jnp.bfloat16)
    return kept + swap(sent, bit, size).astype(jnp.float32)


def add_over(value, size, beside):
    results = []
    for bit in range(size.bit_length() - 1):
        if bit < len(beside):
            operand, product = beside[bit]
            value, operand = lax.optimization_barrier((value, operand))
            result = product(operand)
            other, result = lax.optimization_barrier((swap(value, bit, size), result))
            results.append(result)
        else:
            other = swap(value, bit, size)
        value = value + other
    return value, results + [product(operand) for operand, product in beside[len(results) :]]


def on_device(
    size, tokens, target, norm_gain, up_weight, down_weight, model_codes, hidden_codes
):
    bits = size.bit_length() - 1
    orders = stage_orders(bits)
    own_rows, width = tokens.shape
    total_rows = own_rows * size

    probes = [
        lambda: probe_signs(model_codes[0], hidden_codes[0], D ** (-0.5)),
        lambda: probe_signs(hidden_codes[1], model_codes[1], FF ** (-0.5)),
    ]
    made = []
    own = normalize(tokens, norm_gain)
    halves = [spread(own[:, : width // 2], bits), spread(own[:, width // 2 :], bits)]
    for stage in reversed(range(bits)):
        if stage < 2:
            joined = lax.optimization_barrier((halves[0], halves[1], probes[stage]()))
            halves = [joined[0], joined[1]]
            made.append(joined[2])
        halves = [
            gather_stage(half, order[stage], bits, size) for half, order in zip(halves, orders)
        ]
    probe_down, probe_up = made
    normed = jnp.concatenate([half.reshape(total_rows, width // 2) for half in halves], axis=1)

    preact = jnp.dot(normed, up_weight, preferred_element_type=jnp.float32)
    hidden_f32, first_slope, second_slope = gelu_parts(preact)
    hidden_act = hidden_f32.astype(jnp.bfloat16)
    forward_part = jnp.dot(hidden_act, down_weight, preferred_element_type=jnp.float32)
    forward_sum = scatter_stage(split_rows(forward_part, bits, size), orders[0][0], bits, size)
    tangent = jnp.dot(normed, probe_up, preferred_element_type=jnp.float32)
    hidden_tan = (first_slope * tangent).astype(jnp.bfloat16)
    tangent_part = jnp.dot(
        hidden_tan, down_weight, preferred_element_type=jnp.float32
    ) + jnp.dot(hidden_act, probe_down, preferred_element_type=jnp.float32)
    forward_sum, tangent_part = lax.optimization_barrier((forward_sum, tangent_part))
    tangent_sum = scatter_stage(split_rows(tangent_part, bits, size), orders[1][0], bits, size)
    for stage in range(1, bits):
        forward_sum = scatter_stage(forward_sum, orders[0][stage], bits, size)
        tangent_sum = scatter_stage(tangent_sum, orders[1][stage], bits, size)
    outputs = tokens.astype(jnp.float32) + forward_sum.reshape(own_rows, width)
    doutputs = tangent_sum.reshape(own_rows, width)
    residual_own = ((outputs - target.astype(jnp.float32)) / total_rows).astype(jnp.bfloat16)
    tangent_own = (doutputs / total_rows).astype(jnp.bfloat16)
    residual_all, tangent_all = spread(residual_own, bits), spread(tangent_own, bits)
    hidden = lax.optimization_barrier(jnp.concatenate([hidden_tan, hidden_act], axis=0))
    joined = jnp.zeros((2,) * (bits + 1) + (own_rows, width), jnp.bfloat16)
    for stage in reversed(range(1, bits)):
        if stage == 1:
            joined, residual_all, tangent_all = lax.optimization_barrier(
                (joined, residual_all, tangent_all)
            )
        residual_all = gather_stage(residual_all, orders[0][stage], bits, size)
        tangent_all = gather_stage(tangent_all, orders[1][stage], bits, size)
    blocks = [residual_all, tangent_all]
    others = [swap(block, 0, size) for block in blocks]
    for side, parts in enumerate((blocks, others)):
        for index, part in enumerate(parts):
            start = [index] + [0] * (bits - 1) + [side, 0, 0]
            joined = lax.dynamic_update_slice(joined, part[None], start)
    scaled = lax.optimization_barrier(joined.reshape(2 * total_rows, width))

    back = contract_last(scaled, down_weight)
    back_probe = contract_last(scaled[:total_rows], probe_down)
    back, back_probe = lax.optimization_barrier((back, back_probe))
    back_hidden, back_tangent = back[:total_rows], back[total_rows:]
    curvature = (
        second_slope * tangent * back_hidden + first_slope * (back_tangent + back_probe)
    ).astype(jnp.bfloat16)
    local_sum = jnp.sum(
        tangent * curvature.astype(jnp.float32)
        + hidden_tan.astype(jnp.float32) * (back_probe - back_tangent)
    ) + jnp.sum(doutputs * tangent_own.astype(jnp.float32))
    quadratic_form, (hessian_down, hessian_up) = add_over(
        jnp.reshape(local_sum, (1,)),
        size,
        [
            (hidden, lambda left: contract_first(left, scaled).astype(jnp.bfloat16)),
            (curvature, lambda right: contract_first(normed, right).astype(jnp.bfloat16)),
        ],
    )
    return hessian_up, hessian_down, quadratic_form


def solution(mesh):
    return jax.shard_map(
        functools.partial(on_device, mesh.shape["wide"]),
        mesh=mesh,
        in_specs=(
            P(("groups", "wide"), None),
            P(("groups", "wide"), None),
            P(),
            P(None, "wide"),
            P("wide", None),
            P("groups", None),
            P("groups", "wide"),
        ),
        out_specs=(P("groups", "wide"), P(("groups", "wide"), None), P("groups")),
        check_vma=False,
    )
```

```python
import functools

import jax
import jax.numpy as jnp
from jax import lax
from jax.sharding import PartitionSpec as P

D = 6144
FF = 12288


def normalize(rows, norm_gain):
    wide_rows = rows.astype(jnp.float32)
    center = jnp.mean(wide_rows, axis=1, keepdims=True)
    spread = jnp.mean((wide_rows - center) ** 2, axis=1, keepdims=True)
    return ((wide_rows - center) * lax.rsqrt(spread + 1e-06) * norm_gain).astype(jnp.bfloat16)


def probe_signs(row_codes, column_codes, factor):
    shared = jnp.bitwise_and(row_codes[:, None], column_codes[None, :])
    odd = jnp.bitwise_and(lax.population_count(shared), 1) == 1
    size = jnp.asarray(factor, jnp.float32)
    return jnp.where(odd, -size, size).astype(jnp.bfloat16)


def gelu_parts(preact):
    density = jnp.exp(-0.5 * preact * preact) * 0.3989422804014327
    cumulative = 0.5 * (1.0 + jax.scipy.special.erf(preact * 0.7071067811865476))
    return (preact * cumulative, cumulative + preact * density, density * (2.0 - preact * preact))


def contract_last(left, right):
    return lax.dot_general(
        left, right, (((1,), (1,)), ((), ())), preferred_element_type=jnp.float32
    )


def contract_first(left, right):
    return lax.dot_general(
        left, right, (((0,), (0,)), ((), ())), preferred_element_type=jnp.float32
    )


def swap(value, bit, size):
    pairs = [(i, i ^ (1 << bit)) for i in range(size)]
    return lax.ppermute(value, "wide", pairs)


def stage_orders(bits):
    first = list(range(bits))
    second = list(first)
    if bits > 2:
        second[1], second[2] = first[2], first[1]
    return first, second


def spread(rows, bits):
    return rows.reshape((1,) * bits + rows.shape)


def gather_stage(value, bit, bits, size):
    return lax.concatenate([value, swap(value, bit, size)], bits - 1 - bit)


def split_rows(total, bits, size):
    return total.reshape((2,) * bits + (total.shape[0] // size, total.shape[1]))


def scatter_stage(value, bit, bits, size):
    axis = bits - 1 - bit
    kept = lax.slice_in_dim(value, 0, 1, axis=axis)
    sent = lax.slice_in_dim(value, 1, 2, axis=axis).astype(jnp.bfloat16)
    return kept + swap(sent, bit, size).astype(jnp.float32)


def add_over(value, size, beside):
    results = []
    for bit in range(size.bit_length() - 1):
        if bit < len(beside):
            operand, product = beside[bit]
            value, operand = lax.optimization_barrier((value, operand))
            result = product(operand)
            other, result = lax.optimization_barrier((swap(value, bit, size), result))
            results.append(result)
        else:
            other = swap(value, bit, size)
        value = value + other
    return value, results + [product(operand) for operand, product in beside[len(results) :]]


def on_device(
    size, tokens, target, norm_gain, up_weight, down_weight, model_codes, hidden_codes
):
    bits = size.bit_length() - 1
    orders = stage_orders(bits)
    own_rows, width = tokens.shape
    total_rows = own_rows * size

    probes = [
        lambda: probe_signs(model_codes[0], hidden_codes[0], D ** (-0.5)),
        lambda: probe_signs(hidden_codes[1], model_codes[1], FF ** (-0.5)),
    ]
    made = []
    own = normalize(tokens, norm_gain)
    halves = [spread(own[:, : width // 2], bits), spread(own[:, width // 2 :], bits)]
    for stage in reversed(range(bits)):
        if stage < 2:
            joined = lax.optimization_barrier((halves[0], halves[1], probes[stage]()))
            halves = [joined[0], joined[1]]
            made.append(joined[2])
        halves = [
            gather_stage(half, order[stage], bits, size) for half, order in zip(halves, orders)
        ]
    probe_down, probe_up = made
    normed = jnp.concatenate([half.reshape(total_rows, width // 2) for half in halves], axis=1)

    preact = jnp.dot(normed, up_weight, preferred_element_type=jnp.float32)
    hidden_f32, first_slope, second_slope = gelu_parts(preact)
    hidden_act = hidden_f32.astype(jnp.bfloat16)
    forward_part = jnp.dot(hidden_act, down_weight, preferred_element_type=jnp.float32)
    forward_sum = scatter_stage(split_rows(forward_part, bits, size), orders[0][0], bits, size)
    tangent = jnp.dot(normed, probe_up, preferred_element_type=jnp.float32)
    hidden_tan = (first_slope * tangent).astype(jnp.bfloat16)
    tangent_part = jnp.dot(
        hidden_tan, down_weight, preferred_element_type=jnp.float32
    ) + jnp.dot(hidden_act, probe_down, preferred_element_type=jnp.float32)
    forward_sum, tangent_part = lax.optimization_barrier((forward_sum, tangent_part))
    tangent_sum = scatter_stage(split_rows(tangent_part, bits, size), orders[1][0], bits, size)
    for stage in range(1, bits):
        forward_sum = scatter_stage(forward_sum, orders[0][stage], bits, size)
        tangent_sum = scatter_stage(tangent_sum, orders[1][stage], bits, size)
    outputs = tokens.astype(jnp.float32) + forward_sum.reshape(own_rows, width)
    doutputs = tangent_sum.reshape(own_rows, width)
    residual_own = ((outputs - target.astype(jnp.float32)) / total_rows).astype(jnp.bfloat16)
    tangent_own = (doutputs / total_rows).astype(jnp.bfloat16)
    residual_all, tangent_all = spread(residual_own, bits), spread(tangent_own, bits)
    hidden = lax.optimization_barrier(jnp.concatenate([hidden_tan, hidden_act], axis=0))
    joined = jnp.broadcast_to(
        norm_gain[0].astype(jnp.bfloat16), (2,) * (bits + 1) + (own_rows, width)
    )
    for stage in reversed(range(1, bits)):
        if stage == 1:
            joined, residual_all, tangent_all = lax.optimization_barrier(
                (joined, residual_all, tangent_all)
            )
        residual_all = gather_stage(residual_all, orders[0][stage], bits, size)
        tangent_all = gather_stage(tangent_all, orders[1][stage], bits, size)
    blocks = [residual_all, tangent_all]
    others = [swap(block, 0, size) for block in blocks]
    for side, parts in enumerate((blocks, others)):
        for index, part in enumerate(parts):
            start = [index] + [0] * (bits - 1) + [side, 0, 0]
            joined = lax.dynamic_update_slice(joined, part[None], start)
    scaled = lax.optimization_barrier(joined.reshape(2 * total_rows, width))

    back = contract_last(scaled, down_weight)
    back_probe = contract_last(scaled[:total_rows], probe_down)
    back, back_probe = lax.optimization_barrier((back, back_probe))
    back_hidden, back_tangent = back[:total_rows], back[total_rows:]
    curvature = (
        second_slope * tangent * back_hidden + first_slope * (back_tangent + back_probe)
    ).astype(jnp.bfloat16)
    local_sum = jnp.sum(
        tangent * curvature.astype(jnp.float32)
        + hidden_tan.astype(jnp.float32) * (back_probe - back_tangent)
    ) + jnp.sum(doutputs * tangent_own.astype(jnp.float32))
    quadratic_form, (hessian_up, hessian_down) = add_over(
        jnp.reshape(local_sum, (1,)),
        size,
        [
            (curvature, lambda right: contract_first(normed, right).astype(jnp.bfloat16)),
            (hidden, lambda left: contract_first(left, scaled).astype(jnp.bfloat16)),
        ],
    )
    return hessian_up, hessian_down, quadratic_form


def solution(mesh):
    return jax.shard_map(
        functools.partial(on_device, mesh.shape["wide"]),
        mesh=mesh,
        in_specs=(
            P(("groups", "wide"), None),
            P(("groups", "wide"), None),
            P(),
            P(None, "wide"),
            P("wide", None),
            P("groups", None),
            P("groups", "wide"),
        ),
        out_specs=(P("groups", "wide"), P(("groups", "wide"), None), P("groups")),
        check_vma=False,
    )
```
